256 devices in a mesh: row: 8 (over x, z_hi), col: 32 (over y, z_lo, core).
Axes of the slice: x: 4, y: 4, z: 8 (z_hi: 2, z_lo: 4; z = z_hi * 4 + z_lo), core: 2. Of those that a mesh axis runs over, the one named last changes fastest.
Arguments:
- pair_rep: bfloat16 [1792, 1792, 128], P('row', 'col'), may hold values from -6 to 6
- norm_in: float32 [2, 128], replicated, may hold values from 0.1 to 1.9
- proj_weight: bfloat16 [2, 128, 512], replicated, may hold values from -0.5 to 0.5
- gate_weight: bfloat16 [2, 128, 128], replicated, may hold values from -0.5 to 0.5
- norm_out: float32 [2, 128], replicated, may hold values from 0.1 to 1.9
- out_weight: bfloat16 [2, 128, 128], replicated, may hold values from -0.5 to 0.5
Outputs:
- outgoing: bfloat16 [256, 1792, 128], P(('row', 'col'))
- incoming: bfloat16 [256, 1792, 128], P(('row', 'col'))
The draws below stay inside these ranges and needn't reach their ends.
All inputs are finite; a program needn't handle non-finite values.
Results may differ from the reference program's by a relative error of at most 0.019.
Values may be sent and summed in bfloat16 or wider, within the bound.
A program may use at most 128 MiB of HBM per device.

```python
import jax
import jax.numpy as jnp
from jax import lax

CHANNELS = 128
HIDDEN_SIZE = 128
TOKENS = 1792
STRIDE = 7


def block_levels(own_key, shape, shards, least, high):
    gain = 1.0
    for dim, parts in shards:
        heights = jax.random.uniform(jax.random.fold_in(jax.random.fold_in(own_key, 6), dim), (parts,), jnp.float32, least / len(shards), high / len(shards))
        gain = gain * jnp.repeat(jnp.exp(heights), shape[dim] // parts).reshape((-1,) + (1,) * (len(shape) - 1 - dim))
    return gain


def scatter_about(own_key, dims, deviation, bound, cuts=(), dtype=jnp.bfloat16):
    drawn = jax.random.normal(own_key, dims, jnp.float32) * deviation
    if len(cuts) > 0:
        drawn = block_levels(own_key, dims, cuts, -0.22, 0.18) * drawn
    return jnp.clip(drawn, min=-bound, max=bound).astype(dtype)


def setup_inputs(seed: int = 0) -> dict:
    arg_keys = jax.random.split(jax.random.key(seed), 7)
    pair_rep = scatter_about(arg_keys[0], (TOKENS, TOKENS, CHANNELS), 1.0, 6.0, ((0, 8), (1, 32)))
    norm_in = jnp.clip(1.0 + 0.18 * jax.random.normal(arg_keys[1], (2, CHANNELS), jnp.float32), 0.1, 1.9)
    proj_weight = scatter_about(arg_keys[2], (2, CHANNELS, 4 * HIDDEN_SIZE), CHANNELS ** -0.5, 0.5)
    gate_weight = scatter_about(arg_keys[3], (2, CHANNELS, CHANNELS), CHANNELS ** -0.5, 0.5)
    norm_out = jnp.clip(1.0 + 0.18 * jax.random.normal(arg_keys[4], (2, HIDDEN_SIZE), jnp.float32), 0.1, 1.9)
    out_weight = scatter_about(arg_keys[5], (2, HIDDEN_SIZE, CHANNELS), HIDDEN_SIZE ** -0.5, 0.5)
    return {"pair_rep": pair_rep, "norm_in": norm_in, "proj_weight": proj_weight, "gate_weight": gate_weight, "norm_out": norm_out, "out_weight": out_weight}


def layer_norm(values, scales, along):
    values = values.astype(jnp.float32)
    average = lax.optimization_barrier(jnp.mean(values, axis=along, keepdims=True))
    centered = values - average
    spread = lax.optimization_barrier(jnp.mean(centered * centered, axis=along, keepdims=True))
    return centered * lax.rsqrt(spread + 1e-05) * scales

def to_operand(values):
    rounded = lax.optimization_barrier(values.astype(jnp.bfloat16))
    return rounded.astype(jnp.float32)

def gated(block, scales, weights):
    normed = to_operand(layer_norm(block, scales, 2))
    projected = jnp.einsum('rkc,cg->grk', normed, weights.astype(jnp.float32))
    hidden = weights.shape[1] // 2
    return (jax.nn.sigmoid(projected[:hidden]) * projected[hidden:]).astype(jnp.bfloat16)

def contract(first_op, second_op, pattern):
    groups = HIDDEN_SIZE // 8
    first_groups = first_op.reshape((groups, 8) + first_op.shape[1:])
    second_groups = second_op.reshape((groups, 8) + second_op.shape[1:])

    def product_group(operands):
        return jnp.einsum(pattern, operands[0].astype(jnp.float32), operands[1].astype(jnp.float32))
    result = lax.map(product_group, (first_groups, second_groups))
    return result.reshape((HIDDEN_SIZE,) + result.shape[2:])

def reference(pair_rep, norm_in, proj_weight, gate_weight, norm_out, out_weight):
    row_block = TOKENS // 32
    row_blocks = pair_rep.reshape(32, row_block, TOKENS, CHANNELS)
    band_rows = pair_rep[::STRIDE]
    results = []
    for direction in range(2):
        weights = proj_weight[direction]
        scales = norm_in[direction]
        second_w = weights[:, 2 * HIDDEN_SIZE:]
        pieces = lax.map(lambda span: gated(span, scales, second_w), row_blocks)
        second_full = pieces.transpose(1, 0, 2, 3).reshape(HIDDEN_SIZE, TOKENS, TOKENS)
        if direction == 0:
            first_band = gated(band_rows, scales, weights[:, :2 * HIDDEN_SIZE])
            mixed = contract(first_band, second_full, 'qik,qjk->qij')
        else:
            first_band = gated(pair_rep[:, ::STRIDE], scales, weights[:, :2 * HIDDEN_SIZE])
            mixed = contract(first_band, second_full, 'qki,qkj->qij')
        mixed = mixed.astype(jnp.bfloat16)
        settled = to_operand(layer_norm(mixed, norm_out[direction][:, None, None], 0))
        linear = jnp.einsum('hij,hc->ijc', settled, out_weight[direction].astype(jnp.float32))
        normed_rows = to_operand(layer_norm(band_rows, scales, 2))
        gating = jax.nn.sigmoid(jnp.einsum('ijc,ce->ije', normed_rows, gate_weight[direction].astype(jnp.float32)))
        results.append((gating * linear).astype(jnp.bfloat16))
    return (results[0], results[1])
```

```python
import jax
import jax.numpy as jnp
from jax import lax
from jax.experimental import pallas as pl
from jax.experimental.pallas import tpu as pltpu
from jax.sharding import PartitionSpec as P

MESH = pl.DeviceIdType.MESH
BF = jnp.bfloat16
F32 = jnp.float32

ROWS = 224
COLS = 56
BAND = 32
BCOL = 8
CHUNK = 14
NCH = COLS // CHUNK
EPS = 1e-05


def gate_value(projected):
    gate, value = projected[:128], projected[128:]
    return (0.5 * value) * (1.0 + jnp.tanh(0.5 * gate))


def sigmoid(x):
    return 0.5 + 0.5 * jnp.tanh(0.5 * x)


def unit_norm(x, axis):
    mean = jnp.mean(x, axis=axis, keepdims=True)
    cent = x - mean
    var = jnp.mean(cent * cent, axis=axis, keepdims=True)
    return cent * lax.rsqrt(var + EPS)


def nt(a, b):
    return lax.dot_general(a, b, (((1,), (1,)), ((), ())), preferred_element_type=F32)


def tn(a, b):
    return lax.dot_general(a, b, (((0,), (0,)), ((), ())), preferred_element_type=F32)


def kernel(pair, norm_in, w_t, gate_w, norm_out, out_w, out0, out1,
           xhat, send0, send1, recv0, recv1, f0s, f0r, f1s, f1r, lhs0, lhs1,
           rhs0, rhs1, tmp, part0, rs0, part1, rs1, zsend, zrecv,
           fin0s, fin0r, fin1s, fin1r, grow, g0, g1,
           a2a_s, a2a_r, f_s, f_r, zh_s, zh_r, x_s, x_r, zl_s, zl_r,
           row_s, row_r, rs0_s, rs0_r, rs1_s, rs1_r, rz_s, rz_r,
           fin_s, fin_r, loc):
    r = lax.axis_index("row")
    c = lax.axis_index("col")
    x, zh = r // 2, r % 2
    y, zl, core = c // 8, (c // 2) % 4, c % 2
    yc = y * 2 + core

    def dev(x_, zh_, y_, zl_, core_):
        return (x_ * 2 + zh_, y_ * 8 + zl_ * 2 + core_)

    def dev_yc(o):
        return dev(x, zh, (y + o // 2) % 4, zl, (core + o) % 2)

    def dst_yc(o):
        return ((y + o // 2) % 4) * 2 + (core + o) % 2

    def slot_yc(y_, core_):
        return ((y - y_ + 4) % 4) * 2 + (core - core_ + 2) % 2

    barrier = pltpu.get_barrier_semaphore()

    def greet_col(i, _):
        pl.semaphore_signal(barrier, inc=1, device_id=(r, (c + i) % 32), device_id_type=MESH)
        return 0

    def peer64(i):
        s_, o = (r + i // 8) % 8, i % 8
        return s_, o

    def greet_64(i, _):
        s_, o = peer64(i)
        pl.semaphore_signal(
            barrier, inc=1,
            device_id=(s_, ((y + o // 2) % 4) * 8 + zl * 2 + (core + o) % 2),
            device_id_type=MESH)
        return 0

    lax.fori_loop(1, 32, greet_col, 0)
    lax.fori_loop(8, 64, greet_64, 0)

    def remote(src, dst, ssem, rsem, device):
        return pltpu.make_async_remote_copy(
            src_ref=src, dst_ref=dst, send_sem=ssem, recv_sem=rsem,
            device_id=device, device_id_type=MESH)

    def norm_body(i, _):
        v = pair[pl.ds(i * 4, 4)].astype(F32)
        xhat[pl.ds(i * 4 * COLS, 4 * COLS), :] = unit_norm(v, 2).reshape(4 * COLS, 128)
        return 0

    lax.fori_loop(0, ROWS // 4, norm_body, 0)

    gain0 = norm_in[0:1, :]
    gain1 = norm_in[1:2, :]

    def band_row(u):
        tl = ((u // 2) % 4) * 8 + (u // 8) * 2 + u % 2
        v = xhat[pl.ds(pl.multiple_of(tl * 7 * COLS, 8), COLS), :] * gain0
        return jnp.concatenate([v, jnp.zeros((8, 128), F32)], axis=0)

    def first0_body(i, _):
        rows = jnp.concatenate(
            [band_row(2 * i), band_row(2 * i + 16), band_row(2 * i + 1), band_row(2 * i + 17)],
            axis=0).astype(BF)
        v = gate_value(nt(w_t[0, 0:256, :], rows)).astype(BF)
        f0s[:, 2 * i] = v[:, :128].reshape(8, 16, 128)
        f0s[:, 2 * i + 1] = v[:, 128:].reshape(8, 16, 128)
        return 0

    lax.fori_loop(0, 8, first0_body, 0)

    def column(k, gain):
        v = xhat[pl.ds(k, ROWS, stride=COLS), :] * gain
        return jnp.concatenate([v, jnp.zeros((32, 128), F32)], axis=0).astype(BF)

    def first1_body(b, _):
        v = gate_value(nt(w_t[1, 0:256, :], column(b * 7, gain1))).astype(BF)
        f1s[:, b] = v.reshape(8, 16, 256)
        return 0

    lax.fori_loop(0, BCOL, first1_body, 0)

    pl.semaphore_wait(barrier, 31 + 56)

    def a2a_start(src, dst, ssem, rsem):
        def go(o, _):
            remote(src(dst_yc(o)), dst(o), ssem, rsem, dev_yc(o)).start()
            return 0
        lax.fori_loop(1, 8, go, 0)

    def a2a_wait(src7, dst7, ssem, rsem):
        d = remote(src7, dst7, ssem, rsem, dev_yc(1))
        d.wait_send()
        d.wait_recv()

    a2a_start(lambda d: f0s.at[d], lambda o: f0r.at[o], f_s.at[0], f_r.at[0])
    f0r[0] = f0s[yc]
    a2a_start(lambda d: f1s.at[d], lambda o: f1r.at[o], f_s.at[1], f_r.at[1])
    f1r[0] = f1s[yc]

    def rows_start(i, _):
        cc = (c + i) % 32
        remote(pair.at[cc * 7], grow.at[c], row_s, row_r, (r, cc)).start()
        return 0

    def second(w, gain, send, recv, d):
        for ch in range(NCH):
            def body(k, _):
                v = gate_value(nt(w_t[w, 256:512, :], column(k, gain))).astype(BF)
                send[:, k] = v.reshape(8, 16, 256)
                return 0
            lax.fori_loop(ch * CHUNK, (ch + 1) * CHUNK, body, 0)
            part = pl.ds(ch * CHUNK, CHUNK)
            a2a_start(lambda q: send.at[q, part], lambda o: recv.at[o, part],
                      a2a_s.at[d, ch], a2a_r.at[d, ch])
            recv[0, part] = send[yc, part]

    def second_wait(send, recv, d):
        for ch in range(NCH):
            part = pl.ds(ch * CHUNK, CHUNK)
            a2a_wait(send.at[pl.ds(0, 7), part], recv.at[pl.ds(1, 7), part],
                     a2a_s.at[d, ch], a2a_r.at[d, ch])

    second(0, gain0, send0, recv0, 0)

    a2a_wait(f0s.at[pl.ds(0, 7)], f0r.at[pl.ds(1, 7)], f_s.at[0], f_r.at[0])
    low = lax.broadcasted_iota(jnp.int32, (16 * 16, 128), 1) < 64
    for y_ in range(4):
        a = f0r[slot_yc(y_, 0)].astype(F32).reshape(256, 128)
        b = f0r[slot_yc(y_, 1)].astype(F32).reshape(256, 128)
        tmp[0, 0:256, :] = jnp.where(low, a, pltpu.roll(b, 64, 1))
        tmp[0, 256:512, :] = jnp.where(low, pltpu.roll(a, 64, 1), b)
        for h in range(16):
            lhs0[r, h, :, y_ * 128:(y_ + 1) * 128] = tmp[0, pl.ds(h, 32, stride=16), :].astype(BF)

    zh_copy = remote(lhs0.at[r], lhs0.at[r], zh_s, zh_r, dev(x, 1 - zh, y, zl, core))
    zh_copy.start()
    other = x * 2 + 1 - zh
    x_first = [remote(lhs0.at[r], lhs0.at[r], x_s.at[0, i], x_r.at[0, i],
                      dev((x + i) % 4, zh, y, zl, core)) for i in range(1, 4)]
    for d in x_first:
        d.start()

    a2a_wait(f1s.at[pl.ds(0, 7)], f1r.at[pl.ds(1, 7)], f_s.at[1], f_r.at[1])
    for y_ in range(4):
        for half in range(2):
            lanes = slice(half * 128, half * 128 + 128)
            for cc in range(2):
                tmp[half, cc * 128:cc * 128 + 128, :] = (
                    f1r[slot_yc(y_, cc), :, :, lanes].astype(F32).reshape(128, 128))
            for h in range(16):
                lhs1[zl, h, y_ * 16:(y_ + 1) * 16, lanes] = (
                    tmp[half, pl.ds(h, 16, stride=16), :].astype(BF))
    zl_copies = [remote(lhs1.at[zl], lhs1.at[zl], zl_s.at[i], zl_r.at[i],
                        dev(x, zh, y, (zl + i) % 4, core)) for i in range(1, 4)]
    for d in zl_copies:
        d.start()

    second(1, gain1, send1, recv1, 1)

    lax.fori_loop(1, 32, rows_start, 0)
    grow[c] = pair[c * 7]

    zh_copy.wait_recv()
    x_second = [remote(lhs0.at[other], lhs0.at[other], x_s.at[1, i], x_r.at[1, i],
                       dev((x + i) % 4, zh, y, zl, core)) for i in range(1, 4)]
    for d in x_second:
        d.start()

    def spread(recv, y_):
        def body(i, _):
            for cc in range(2):
                v = recv[slot_yc(y_, cc), pl.ds(i * 8, 8)].astype(F32).reshape(128, 256)
                at = pl.ds(pl.multiple_of(cc * 896 + i * 128, 128), 128)
                tmp[0, at, :] = v[:, :128]
                tmp[1, at, :] = v[:, 128:]
            return 0
        lax.fori_loop(0, 7, body, 0)

    second_wait(send0, recv0, 0)
    pad8 = jnp.zeros((8, 128), F32)
    for y_ in range(4):
        spread(recv0, y_)

        def body(h, _):
            for half in range(2):
                v = jnp.concatenate(
                    [tmp[half, pl.ds(h, 56, stride=16), :], pad8,
                     tmp[half, pl.ds(h + 896, 56, stride=16), :], pad8], axis=0)
                rhs0[h, y_ * 128:(y_ + 1) * 128, half * 128:half * 128 + 128] = v.astype(BF)
            return 0
        lax.fori_loop(0, 16, body, 0)

    for d in x_first + x_second:
        d.wait_recv()

    def product0(h, _):
        a = lhs0[:, h].reshape(256, 512)
        v = jnp.dot(a, rhs0[h], preferred_element_type=F32).astype(F32).reshape(8, 4, 8, 256)
        for q in range(4):
            part0[q, h] = v[:, q].reshape(64, 256).astype(BF)
        return 0

    lax.fori_loop(0, 16, product0, 0)
    rs0_copies = [remote(part0.at[(zl + i) % 4], rs0.at[i - 1], rs0_s.at[i], rs0_r.at[i],
                         dev(x, zh, y, (zl + i) % 4, core)) for i in range(1, 4)]
    for d in rs0_copies:
        d.start()

    second_wait(send1, recv1, 1)
    for y_ in range(4):
        spread(recv1, y_)

        def body(h, _):
            for half in range(2):
                rhs1[h, y_ * 112:(y_ + 1) * 112, half * 128:half * 128 + 128] = (
                    tmp[half, pl.ds(h, 112, stride=16), :].astype(BF))
            return 0
        lax.fori_loop(0, 16, body, 0)
    for d in zl_copies:
        d.wait_recv()

    def product1(h, _):
        a = lhs1[:, h].reshape(256, 256)
        v = nt(a, rhs1[h]).reshape(4, 4, 16, 448)
        for q in range(4):
            part1[q, h] = v[:, q].reshape(64, 448).astype(BF)
        return 0

    lax.fori_loop(0, 16, product1, 0)
    rs1_copies = [remote(part1.at[(x + i) % 4], rs1.at[i - 1], rs1_s.at[i], rs1_r.at[i],
                         dev((x + i) % 4, zh, y, zl, core)) for i in range(1, 4)]
    for d in rs1_copies:
        d.start()

    rows_all = remote(grow.at[pl.ds(0, 31)], grow.at[pl.ds(0, 31)], row_s, row_r, (r, (c + 1) % 32))
    rows_all.wait_send()
    rows_all.wait_recv()

    def gates(i, _):
        v = unit_norm(grow[pl.ds(i * 4, 4)].astype(F32), 2).reshape(4 * COLS, 128)
        at = pl.ds(pl.multiple_of(i * 4 * COLS, 8), 4 * COLS)
        g0[at, :] = sigmoid(jnp.dot((v * gain0).astype(BF), gate_w[0], preferred_element_type=F32))
        g1[at, :] = sigmoid(jnp.dot((v * gain1).astype(BF), gate_w[1], preferred_element_type=F32))
        return 0

    lax.fori_loop(0, 8, gates, 0)

    for d in rs0_copies:
        d.wait_recv()

    def sum0(h, _):
        v = part0[zl, h].astype(F32)
        for i in range(3):
            v = v + rs0[i, h].astype(F32)
        at = pl.ds(pl.multiple_of(h * 64, 64), 64)
        tmp[0, at, :] = v[:, :128]
        tmp[1, at, :] = v[:, 128:]
        return 0

    lax.fori_loop(0, 16, sum0, 0)

    def turn0(t, _):
        fin0s[t] = jnp.concatenate(
            [tmp[half, pl.ds(t, 16, stride=64), :] for half in range(2)], axis=1).astype(BF)
        return 0

    lax.fori_loop(0, 64, turn0, 0)
    me64 = r * 8 + yc

    def fin0_start(i, _):
        s_, o = peer64(i)
        q = dst_yc(o)
        remote(fin0s.at[s_ * 8 + q], fin0r.at[me64], fin_s.at[0], fin_r.at[0],
               (s_, (q // 2) * 8 + zl * 2 + q % 2)).start()
        return 0

    lax.fori_loop(1, 64, fin0_start, 0)
    fin0r[me64] = fin0s[me64]

    for d in rs1_copies:
        d.wait_recv()

    def sum1(h, _):
        v = part1[x, h].astype(F32)
        for i in range(3):
            v = v + rs1[i, h].astype(F32)
        v = v.astype(BF)
        zsend[0, h] = v[:32]
        zsend[1, h] = v[32:]
        return 0

    lax.fori_loop(0, 16, sum1, 0)
    rz = remote(zsend.at[1 - zh], zrecv, rz_s, rz_r, dev(x, 1 - zh, y, zl, core))
    rz.start()

    fin0_all = remote(fin0s.at[pl.ds(0, 63)], fin0r.at[pl.ds(0, 63)], fin_s.at[0], fin_r.at[0], dev_yc(1))
    fin0_all.wait_send()
    fin0_all.wait_recv()

    def settle(v, d):
        return (unit_norm(v.astype(F32), 0) * norm_out[d]).astype(BF)

    def finish0(s, _):
        v = fin0r[pl.ds(s * 8, 8)].reshape(128, 256)
        linear = tn(settle(v, 0), out_w[0])[:ROWS]
        at = pl.ds(pl.multiple_of(s * ROWS, 8), ROWS)
        out0[0, pl.ds(pl.multiple_of(s * ROWS, 16), ROWS), :] = (g0[at, :] * linear).astype(BF)
        return 0

    lax.fori_loop(0, 8, finish0, 0)

    rz.wait_recv()

    def sum2(h, _):
        v = zsend[zh, h].astype(F32) + zrecv[h].astype(F32)
        at = pl.ds(pl.multiple_of(h * 32, 32), 32)
        for q in range(3):
            tmp[q // 2, pl.ds(pl.multiple_of((q % 2) * 512 + h * 32, 32), 32), :] = v[:, q * 128:(q + 1) * 128]
        tmp[1, pl.ds(pl.multiple_of(512 + h * 32, 32), 32), :] = jnp.concatenate(
            [v[:, 384:], jnp.zeros((32, 64), F32)], axis=1)
        return 0

    lax.fori_loop(0, 16, sum2, 0)

    def turn1(t, _):
        v = jnp.concatenate(
            [tmp[q // 2, pl.ds((q % 2) * 512 + t, 16, stride=32), :] for q in range(4)], axis=1)
        fin1s[t] = v[:, :448].astype(BF)
        return 0

    lax.fori_loop(0, 32, turn1, 0)

    def fin1_start(i, _):
        cc = (c + i) % 32
        remote(fin1s.at[cc], fin1r.at[c], fin_s.at[1], fin_r.at[1], (r, cc)).start()
        return 0

    lax.fori_loop(1, 32, fin1_start, 0)
    fin1r[c] = fin1s[c]
    fin1_all = remote(fin1s.at[pl.ds(0, 31)], fin1r.at[pl.ds(0, 31)], fin_s.at[1], fin_r.at[1], dev_yc(1))
    fin1_all.wait_send()
    fin1_all.wait_recv()

    for z_ in range(4):
        v = jnp.concatenate(
            [fin1r[y_ * 8 + z_ * 2 + cc] for y_ in range(4) for cc in range(2)], axis=0)
        linear = tn(settle(v, 1), out_w[1])
        for y_ in range(4):
            at = (y_ * 8 + z_ * 2) * COLS
            out1[0, at:at + 112, :] = (
                g1[at:at + 112, :] * linear[y_ * 112:(y_ + 1) * 112]).astype(BF)

    zh_copy.wait_send()
    rz.wait_send()
    for d in x_first + x_second + zl_copies + rs0_copies + rs1_copies:
        d.wait_send()


def shards(pair_rep, norm_in, proj_weight, gate_weight, norm_out, out_weight):
    w_t = jnp.swapaxes(proj_weight, 1, 2)
    vm = pl.BlockSpec(memory_space=pltpu.VMEM)
    dma = pltpu.SemaphoreType.DMA
    V = pltpu.VMEM
    return pl.pallas_call(
        kernel,
        name="triangles",
        out_shape=[jax.ShapeDtypeStruct((1, 1792, 128), BF)] * 2,
        in_specs=[vm] * 6,
        out_specs=[vm] * 2,
        scratch_shapes=[
            V((ROWS * COLS, 128), F32),
            V((8, COLS, 16, 256), BF), V((8, COLS, 16, 256), BF),
            V((8, COLS, 16, 256), BF), V((8, COLS, 16, 256), BF),
            V((8, 16, 16, 128), BF), V((8, 16, 16, 128), BF),
            V((8, 8, 16, 256), BF), V((8, 8, 16, 256), BF),
            V((8, 16, 32, 512), BF), V((4, 16, 64, 256), BF),
            V((16, 512, 256), BF), V((16, 448, 256), BF),
            V((2, 1792, 128), F32),
            V((4, 16, 64, 256), BF), V((3, 16, 64, 256), BF),
            V((4, 16, 64, 448), BF), V((3, 16, 64, 448), BF),
            V((2, 16, 32, 448), BF), V((16, 32, 448), BF),
            V((64, 16, 256), BF), V((64, 16, 256), BF),
            V((32, 16, 448), BF), V((32, 16, 448), BF),
            V((32, COLS, 128), BF), V((1792, 128), F32), V((1792, 128), F32),
            dma((2, NCH)), dma((2, NCH)), dma((2,)), dma((2,)), dma, dma,
            dma((2, 4)), dma((2, 4)), dma((4,)), dma((4,)),
            dma, dma, dma((4,)), dma((4,)), dma((4,)), dma((4,)), dma, dma,
            dma((2,)), dma((2,)), dma,
        ],
        compiler_params=pltpu.CompilerParams(
            collective_id=0, has_side_effects=True, vmem_limit_bytes=60 << 20),
    )(pair_rep, norm_in, w_t, gate_weight, norm_out[:, :, None], out_weight)


def solution(mesh):
    in_specs = (P("row", "col", None), P(), P(), P(), P(), P())
    out_specs = (P(("row", "col"), None, None), P(("row", "col"), None, None))
    return jax.shard_map(shards, mesh=mesh, in_specs=in_specs, out_specs=out_specs, check_vma=False)
```

```python
import jax
import jax.numpy as jnp
from jax import lax
from jax.experimental import pallas as pl
from jax.experimental.pallas import tpu as pltpu
from jax.sharding import PartitionSpec as P

MESH = pl.DeviceIdType.MESH
BF = jnp.bfloat16
F32 = jnp.float32

ROWS = 224
COLS = 56
EPS = 1e-05
TILES = 25
CUTS = ((0, 4, 0, 14), (4, 7, 14, 25))
WIDE = 16


def gate_value(projected):
    gate, value = projected[:256], projected[256:]
    return (0.5 * value) * (1.0 + jnp.tanh(0.5 * gate))


def sigmoid(x):
    return 0.5 + 0.5 * jnp.tanh(0.5 * x)


def unit_norm(x, axis):
    mean = jnp.mean(x, axis=axis, keepdims=True)
    cent = x - mean
    var = jnp.mean(cent * cent, axis=axis, keepdims=True)
    return cent * lax.rsqrt(var + EPS)


def nt(a, b):
    return lax.dot_general(a, b, (((1,), (1,)), ((), ())), preferred_element_type=F32)


def tn(a, b):
    return lax.dot_general(a, b, (((0,), (0,)), ((), ())), preferred_element_type=F32)


def lane_of(v):
    return lax.broadcasted_iota(jnp.int32, v.shape, len(v.shape) - 1)


def roll(v, by):
    return pltpu.roll(v, by, len(v.shape) - 1)


def unpack(t0, t1, t2):
    lane = lane_of(t0)
    zero = jnp.zeros_like(t0)
    parts = (t0, roll(jnp.where(lane < 64, t1, t0), 32),
             roll(jnp.where(lane < 32, t2, t1), 64), roll(t2, 96))
    return [jnp.where(lane < 96, p, zero) for p in parts]


def kernel(pair, norm_in, w, gate_w, norm_out, out_w, out0, out1,
           xhat, wb, send0, send1, recv0, recv1, f0s, f0r, f1s, f1r, lhs0, lhs1,
           rhs0, rhs1, tmp, part0, rs0, part1, zrecv, xs, xr,
           fin0s, fin0r, fin1s, fin1r, grow, g0, g1,
           a2a_s, a2a_r, f_s, f_r, zh_s, zh_r, zl_s, zl_r,
           row_s, row_r, rs0_s, rs0_r, rz_s, rz_r, xa_s, xa_r, fin_s, fin_r):
    r = lax.axis_index("row")
    c = lax.axis_index("col")
    x, zh = r // 2, r % 2
    y, zl, core = c // 8, (c // 2) % 4, c % 2
    me = (y * 2 + core) * 4 + x
    me64 = zh * 32 + me

    def dev(x_, zh_, y_, zl_, core_):
        return (x_ * 2 + zh_, y_ * 8 + zl_ * 2 + core_)

    def dev64(e):
        return dev(e % 4, e // 32, (e // 8) % 4, zl, (e // 4) % 2)

    barrier = pltpu.get_barrier_semaphore()

    def greet_64(i, _):
        pl.semaphore_signal(barrier, inc=1, device_id=dev64((me64 + i) % 64), device_id_type=MESH)
        return 0

    def greet_zl(i, _):
        pl.semaphore_signal(
            barrier, inc=1, device_id=dev(x, zh, (i // 2) % 4, (zl + i // 8) % 4, i % 2),
            device_id_type=MESH)
        return 0

    lax.fori_loop(1, 64, greet_64, 0)
    lax.fori_loop(8, 32, greet_zl, 0)

    def remote(src, dst, ssem, rsem, device):
        return pltpu.make_async_remote_copy(
            src_ref=src, dst_ref=dst, send_sem=ssem, recv_sem=rsem,
            device_id=device, device_id_type=MESH)

    gain0 = norm_in[0:1, :]
    gain1 = norm_in[1:2, :]
    near = dev(x, 1 - zh, y, zl, core)

    sub = lax.broadcasted_iota(jnp.int32, (16, 8, 128), 1)
    none = jnp.zeros((16, 8, 128), F32)

    def weights(d, which):
        for part in range(2):
            at = which * 256 + part * 128
            t = w[d, :, at:at + 128].astype(F32).T.reshape(16, 8, 128)
            turned = pltpu.roll(t, 4, 1)
            even = jnp.concatenate(
                [jnp.where(sub < 4, t, none), jnp.where(sub < 4, none, turned)], axis=2)
            odd = jnp.concatenate(
                [jnp.where(sub < 4, turned, none), jnp.where(sub < 4, none, t)], axis=2)
            both = jnp.concatenate([even[:, None], odd[:, None]], axis=1)
            wb[d, which, part * 256:part * 256 + 256, :] = both.reshape(256, 256).astype(BF)

    weights(0, 0)
    weights(1, 0)
    weights(0, 1)
    weights(1, 1)

    def norm_body(i, _):
        n = WIDE * COLS
        v = pair[pl.ds(i * WIDE, WIDE)].astype(F32).reshape(n, 128)
        xhat[pl.ds(pl.multiple_of(i * n, 8), n), :] = unit_norm(v, 1)
        return 0

    lax.fori_loop(0, ROWS // WIDE, norm_body, 0)

    pad = jnp.zeros((8, 128), F32)

    def band_rows(p):
        rows = []
        for u in (p, p + 16):
            tl = ((u // 2) % 4) * 8 + (u // 8) * 2 + u % 2
            rows += [xhat[tl * 7 * COLS:tl * 7 * COLS + COLS, :] * gain0, pad]
        return jnp.concatenate(rows, axis=0).astype(BF)

    def pairs(a, b):
        return jnp.concatenate([a, b], axis=1)

    def stack(a, b):
        n = a.shape[1]
        return jnp.concatenate([a.reshape(32, 8, n), b.reshape(32, 8, n)], axis=1).astype(BF)

    for i in range(4):
        rows = jnp.concatenate(
            [pairs(band_rows(4 * i), band_rows(4 * i + 1)),
             pairs(band_rows(4 * i + 2), band_rows(4 * i + 3))], axis=0)
        v = gate_value(nt(wb[0, 0], rows))
        f0s[:, i] = stack(v[:, :128], v[:, 128:])

    def column(k, gain):
        return xhat[pl.ds(k, ROWS, stride=COLS), :] * gain

    pad32 = jnp.zeros((32, 256), F32)
    for i in range(2):
        v = []
        for j in range(2):
            b = 4 * i + 2 * j
            rows = pairs(column(7 * b, gain1), column(7 * b + 7, gain1))
            v.append(gate_value(nt(wb[1, 0], jnp.concatenate([rows, pad32], axis=0).astype(BF))))
        f1s[:, i] = stack(v[0], v[1])

    pl.semaphore_wait(barrier, 87)

    def a2a_start(src, dst, ssem, rsem):
        def go(i, _):
            e = (me + i) % 32
            remote(src(e), dst, ssem, rsem, dev(e % 4, zh, e // 8, zl, (e // 4) % 2)).start()
            return 0
        lax.fori_loop(1, 32, go, 0)

    def all_wait(src, dst, ssem, rsem):
        d = remote(src, dst, ssem, rsem, near)
        d.wait_send()
        d.wait_recv()

    a2a_start(lambda e: f0s.at[e], f0r.at[me], f_s.at[0], f_r.at[0])
    f0r[me] = f0s[me]
    a2a_start(lambda e: f1s.at[e], f1r.at[me], f_s.at[1], f_r.at[1])
    f1r[me] = f1s[me]

    def rows_start(i, _):
        cc = (c + i) % 32
        remote(pair.at[cc * 7], grow.at[c], row_s, row_r, (r, cc)).start()
        return 0

    lax.fori_loop(1, 32, rows_start, 0)
    grow[c] = pair[c * 7]

    def second(d, gain, send, recv):
        def group(k):
            low, high = [], []
            for j in range(4):
                v = pairs(column(k * 8 + 2 * j, gain), column(k * 8 + 2 * j + 1, gain))
                low.append(v[:128])
                high.append(v[128:])
            rows = jnp.concatenate(low + high, axis=0).astype(BF)
            v = gate_value(nt(wb[d, 1], rows))
            return [v[:, n * 128:(n + 1) * 128] for n in range(7)]

        for ch, (first, last, t0, t1) in enumerate(CUTS):
            for k in range((last - first) // 2):
                at = t0 + 7 * k
                blocks = group(first + 2 * k) + group(first + 2 * k + 1)
                for n in range(7):
                    send[:, at + n] = stack(blocks[2 * n], blocks[2 * n + 1])
            if (last - first) % 2:
                blocks = group(last - 1)
                blocks.append(jnp.zeros_like(blocks[0]))
                for n in range(4):
                    send[:, t1 - 4 + n] = stack(blocks[2 * n], blocks[2 * n + 1])
            part = pl.ds(t0, t1 - t0)
            a2a_start(lambda e: send.at[e, part], recv.at[me, part], a2a_s.at[d, ch], a2a_r.at[d, ch])
            recv[me, part] = send[me, part]

    def second_wait(d, send, recv):
        for ch, (_, _, t0, t1) in enumerate(CUTS):
            part = pl.ds(t0, t1 - t0)
            all_wait(send.at[pl.ds(0, 31), part], recv.at[pl.ds(0, 31), part],
                     a2a_s.at[d, ch], a2a_r.at[d, ch])

    second(0, gain0, send0, recv0)

    all_wait(f0s.at[pl.ds(0, 31)], f0r.at[pl.ds(0, 31)], f_s.at[0], f_r.at[0])
    for x_ in range(4):
        for y_ in range(4):
            a = f0r[y_ * 8 + x_].astype(F32).reshape(64, 128)
            b = f0r[y_ * 8 + 4 + x_].astype(F32).reshape(64, 128)
            low = lane_of(a) < 64
            tmp[0, 0:64, :] = jnp.where(low, a, roll(b, 64))
            tmp[0, 64:128, :] = jnp.where(low, roll(a, 64), b)
            for h in range(4):
                lhs0[zh, h, x_ * 32:(x_ + 1) * 32, y_ * 128:(y_ + 1) * 128] = (
                    tmp[0, pl.ds(h, 32, stride=4), :].astype(BF))
    zh_copy = remote(lhs0.at[zh], lhs0.at[zh], zh_s, zh_r, near)
    zh_copy.start()

    all_wait(f1s.at[pl.ds(0, 31)], f1r.at[pl.ds(0, 31)], f_s.at[1], f_r.at[1])
    for x_ in range(4):
        for y_ in range(4):
            for half in range(2):
                lanes = slice(half * 128, half * 128 + 128)
                for cc in range(2):
                    tmp[half, cc * 32:cc * 32 + 32, :] = (
                        f1r[y_ * 8 + cc * 4 + x_, :, :, lanes].astype(F32).reshape(32, 128))
                for h in range(4):
                    at = x_ * 256 + half * 128
                    lhs1[zl, h, y_ * 16:(y_ + 1) * 16, at:at + 128] = (
                        tmp[half, pl.ds(h, 16, stride=4), :].astype(BF))
    zl_copies = [remote(lhs1.at[zl], lhs1.at[zl], zl_s.at[i], zl_r.at[i],
                        dev(x, zh, y, (zl + i) % 4, core)) for i in range(1, 4)]
    for d in zl_copies:
        d.start()

    second(1, gain1, send1, recv1)

    all_wait(grow.at[pl.ds(0, 31)], grow.at[pl.ds(0, 31)], row_s, row_r)

    def gates(i, _):
        v = unit_norm(grow[pl.ds(i * 4, 4)].astype(F32).reshape(4 * COLS, 128), 1)
        at = pl.ds(pl.multiple_of(i * 4 * COLS, 8), 4 * COLS)
        g0[at, :] = sigmoid(jnp.dot((v * gain0).astype(BF), gate_w[0], preferred_element_type=F32))
        g1[at, :] = sigmoid(jnp.dot((v * gain1).astype(BF), gate_w[1], preferred_element_type=F32))
        return 0

    lax.fori_loop(0, 8, gates, 0)

    def spread(recv, x_, y_):
        for cc in range(2):
            v = recv[y_ * 8 + cc * 4 + x_].astype(F32).reshape(50, 8, 128)
            for k in range(7):
                at = cc * 224 + k * 32
                n = k * 7
                tmp[0, at:at + 32, :] = v[n:n + 4].reshape(32, 128)
                for j, q in enumerate(unpack(v[n + 4], v[n + 5], v[n + 6])):
                    tmp[1, at + j * 8:at + j * 8 + 8, :] = q

    second_wait(0, send0, recv0)

    def spread0(i, _):
        x_, y_ = i % 4, i // 4
        spread(recv0, x_, y_)
        for h in range(4):
            for half in range(2):
                v = jnp.concatenate(
                    [tmp[half, pl.ds(h, 56, stride=4), :], pad,
                     tmp[half, pl.ds(h + 224, 56, stride=4), :], pad], axis=0)
                rhs0[h * 4 + x_, pl.ds(pl.multiple_of(y_ * 128, 128), 128),
                     half * 128:half * 128 + 128] = v.astype(BF)
        return 0

    lax.fori_loop(0, 16, spread0, 0)
    zh_copy.wait_recv()

    def product0(i, _):
        a = lhs0[:, i // 4].reshape(256, 512)
        v = jnp.dot(a, rhs0[i], preferred_element_type=F32).reshape(8, 4, 8, 256)
        for q in range(4):
            part0[q, i] = v[:, q].reshape(64, 256).astype(BF)
        return 0

    lax.fori_loop(0, 16, product0, 0)
    rs0_copies = [remote(part0.at[(zl + i) % 4], rs0.at[i - 1], rs0_s.at[i], rs0_r.at[i],
                         dev(x, zh, y, (zl + i) % 4, core)) for i in range(1, 4)]
    for d in rs0_copies:
        d.start()

    second_wait(1, send1, recv1)

    def spread1(i, _):
        x_, y_ = i % 4, i // 4
        spread(recv1, x_, y_)
        for h in range(4):
            for half in range(2):
                at = pl.multiple_of(x_ * 256 + half * 128, 128)
                rhs1[h, pl.ds(pl.multiple_of(y_ * 112, 16), 112), pl.ds(at, 128)] = (
                    tmp[half, pl.ds(h, 112, stride=4), :].astype(BF))
        return 0

    lax.fori_loop(0, 16, spread1, 0)
    for d in zl_copies:
        d.wait_recv()

    def product1(h, _):
        a = lhs1[:, h].reshape(256, 1024)
        v = nt(a, rhs1[h]).reshape(2, 2, 4, 16, 448)
        for q in range(2):
            for x_ in range(4):
                part1[q, h, x_ * 32:(x_ + 1) * 32, :] = v[q, :, x_].reshape(32, 448).astype(BF)
        return 0

    lax.fori_loop(0, 4, product1, 0)
    rz = remote(part1.at[1 - zh], zrecv, rz_s, rz_r, near)
    rz.start()

    rz.wait_recv()

    def sum1(h, _):
        v = part1[zh, h].astype(F32) + zrecv[h].astype(F32)
        for x_ in range(4):
            xs[x_, h] = v[x_ * 32:(x_ + 1) * 32].astype(BF)
        return 0

    lax.fori_loop(0, 4, sum1, 0)
    x_copies = [remote(xs.at[(x + i) % 4], xr.at[x], xa_s.at[i], xa_r.at[i],
                       dev((x + i) % 4, zh, y, zl, core)) for i in range(1, 4)]
    for d in x_copies:
        d.start()
    xr[x] = xs[x]

    for d in rs0_copies:
        d.wait_recv()

    def sum0(h, _):
        v = part0[zl, h].astype(F32)
        for i in range(3):
            v = v + rs0[i, h].astype(F32)
        at = pl.ds(pl.multiple_of(h * 64, 64), 64)
        tmp[0, at, :] = v[:, :128]
        tmp[1, at, :] = v[:, 128:]
        return 0

    lax.fori_loop(0, 16, sum0, 0)

    def turn0(t, _):
        fin0s[t] = jnp.concatenate(
            [tmp[half, pl.ds(t, 16, stride=64), :] for half in range(2)], axis=1).astype(BF)
        return 0

    lax.fori_loop(0, 64, turn0, 0)

    def row64(e):
        return (e // 32) * 32 + (e % 4) * 8 + (e // 4) % 8

    def fin0_start(i, _):
        e = (me64 + i) % 64
        remote(fin0s.at[row64(e)], fin0r.at[me64], fin_s.at[0], fin_r.at[0], dev64(e)).start()
        return 0

    lax.fori_loop(1, 64, fin0_start, 0)
    fin0r[me64] = fin0s[row64(me64)]

    for d in x_copies:
        d.wait_recv()

    def fill1(h, _):
        v = xr[h // 4, h % 4].astype(F32)
        for q in range(4):
            part = v[:, q * 128:(q + 1) * 128] if q < 3 else jnp.concatenate(
                [v[:, 384:], jnp.zeros((32, 64), F32)], axis=1)
            tmp[q // 2, pl.ds(pl.multiple_of((q % 2) * 512 + h * 32, 32), 32), :] = part
        return 0

    lax.fori_loop(0, 16, fill1, 0)

    def turn1(t, _):
        v = jnp.concatenate(
            [tmp[q // 2, pl.ds((q % 2) * 512 + t, 16, stride=32), :] for q in range(4)], axis=1)
        fin1s[t] = v[:, :448].astype(BF)
        return 0

    lax.fori_loop(0, 32, turn1, 0)

    def fin1_start(i, _):
        cc = (c + i) % 32
        remote(fin1s.at[cc], fin1r.at[c], fin_s.at[1], fin_r.at[1], (r, cc)).start()
        return 0

    lax.fori_loop(1, 32, fin1_start, 0)
    fin1r[c] = fin1s[c]

    all_wait(fin0s.at[pl.ds(0, 63)], fin0r.at[pl.ds(0, 63)], fin_s.at[0], fin_r.at[0])

    def settle(v, d):
        return (unit_norm(v, 0) * norm_out[d]).astype(BF)

    for z_ in range(2):
        v = fin0r[z_ * 32:z_ * 32 + 32].astype(F32).reshape(512, 256)
        tmp[0, 0:512, :] = v[:, :128]
        tmp[1, 0:512, :] = v[:, 128:]
        for x_ in range(4):
            v = jnp.concatenate([tmp[half, pl.ds(x_, 128, stride=4), :] for half in range(2)], axis=1)
            linear = tn(settle(v, 0), out_w[0])[:ROWS]
            at = (x_ * 2 + z_) * ROWS
            out0[0, at:at + ROWS, :] = (g0[at:at + ROWS, :] * linear).astype(BF)

    all_wait(fin1s.at[pl.ds(0, 31)], fin1r.at[pl.ds(0, 31)], fin_s.at[1], fin_r.at[1])
    for z_ in range(4):
        v = jnp.concatenate(
            [fin1r[y_ * 8 + z_ * 2 + cc] for y_ in range(4) for cc in range(2)], axis=0)
        linear = tn(settle(v.astype(F32), 1), out_w[1])
        for y_ in range(4):
            at = (y_ * 8 + z_ * 2) * COLS
            out1[0, at:at + 112, :] = (
                g1[at:at + 112, :] * linear[y_ * 112:(y_ + 1) * 112]).astype(BF)

    zh_copy.wait_send()
    rz.wait_send()
    for d in zl_copies + rs0_copies + x_copies:
        d.wait_send()


def shards(pair_rep, norm_in, proj_weight, gate_weight, norm_out, out_weight):
    vm = pl.BlockSpec(memory_space=pltpu.VMEM)
    dma = pltpu.SemaphoreType.DMA
    V = pltpu.VMEM
    return pl.pallas_call(
        kernel,
        name="triangles",
        out_shape=[jax.ShapeDtypeStruct((1, 1792, 128), BF)] * 2,
        in_specs=[vm] * 6,
        out_specs=[vm] * 2,
        scratch_shapes=[
            V((ROWS * COLS, 128), F32), V((2, 2, 512, 256), BF),
            V((32, TILES, 16, 128), BF), V((32, TILES, 16, 128), BF),
            V((32, TILES, 16, 128), BF), V((32, TILES, 16, 128), BF),
            V((32, 4, 16, 128), BF), V((32, 4, 16, 128), BF),
            V((32, 2, 16, 256), BF), V((32, 2, 16, 256), BF),
            V((2, 4, 128, 512), BF), V((4, 4, 64, 1024), BF),
            V((16, 512, 256), BF), V((4, 448, 1024), BF),
            V((2, 1024, 128), F32),
            V((4, 16, 64, 256), BF), V((3, 16, 64, 256), BF),
            V((2, 4, 128, 448), BF), V((4, 128, 448), BF),
            V((4, 4, 32, 448), BF), V((4, 4, 32, 448), BF),
            V((64, 16, 256), BF), V((64, 16, 256), BF),
            V((32, 16, 448), BF), V((32, 16, 448), BF),
            V((32, COLS, 128), BF), V((1792, 128), F32), V((1792, 128), F32),
            dma((2, 2)), dma((2, 2)), dma((2,)), dma((2,)), dma, dma,
            dma((4,)), dma((4,)), dma, dma, dma((4,)), dma((4,)), dma, dma,
            dma((4,)), dma((4,)), dma((2,)), dma((2,)),
        ],
        compiler_params=pltpu.CompilerParams(
            collective_id=0, has_side_effects=True, vmem_limit_bytes=60 << 20),
    )(pair_rep, norm_in, proj_weight, gate_weight, norm_out[:, :, None], out_weight)


def solution(mesh):
    in_specs = (P("row", "col", None), P(), P(), P(), P(), P())
    out_specs = (P(("row", "col"), None, None), P(("row", "col"), None, None))
    return jax.shard_map(shards, mesh=mesh, in_specs=in_specs, out_specs=out_specs, check_vma=False)
```
